32 devices in a mesh: tm: 4 (over z), rows: 8 (over y, x, core).
Axes of the slice: x: 2, y: 2, z: 4, core: 2. Of those that a mesh axis runs over, the one named last changes fastest.
Arguments:
- features: bfloat16 [4, 128, 64, 256], P('tm', 'rows'), may hold values from -6 to 6
- block_shift: int32 [3, 4, 4, 16, 32], P(None, None, 'tm', 'rows'), may hold values from -5 to 5
- quarter_pel: int32 [3, 4, 4, 16, 32], P(None, None, 'tm', 'rows'), may hold values from 0 to 3
- update_mask: int32 [3, 4], P(None, 'tm'), may hold values 0 or 1
- uniting_weight: bfloat16 [3, 3, 64, 192], replicated, may hold values from -0.15625 to 0.15625
- mixing_weight: bfloat16 [3, 3, 64, 64], replicated, may hold values from -0.25 to 0.25
Outputs:
- refined: bfloat16 [4, 128, 64, 256], P('tm', 'rows')
The draws below stay inside these ranges and needn't reach their ends.
All inputs are finite; a program needn't handle non-finite values. No bound on the sum of `update_mask` on one device may be relied on, other than what follows from the above.
Results may differ from the reference program's by a relative error of at most 0.0057.
Values may be sent and summed in bfloat16 or wider, within the bound.
A program may use at most 128 MiB of HBM per device.

```python
import jax
import jax.numpy as jnp
from jax import lax

CH = 64
WIDTH = 256
LEVELS = 3
SPAN = 5
FRAMES = 4
HEIGHT = 128


def place_ends(drawn, stream_key, smallest, high):
    longest = drawn.shape.index(max(drawn.shape))
    spots = []
    for shift in (0, 1):
        where = [jax.random.randint(jax.random.fold_in(stream_key, axis), (), 0, length) for axis, length in enumerate(drawn.shape)]
        where[longest] = (where[longest] + shift) % drawn.shape[longest]
        spots.append(tuple(where))
    return drawn.at[spots[0]].set(smallest).at[spots[1]].set(high)


def shard_levels(key, dims, pieces, low, high):
    def one(dim, shards_of):
        heights = jax.random.uniform(jax.random.fold_in(jax.random.fold_in(key, 6), dim), (shards_of,), jnp.float32, low / len(pieces), high / len(pieces))
        return jnp.repeat(jnp.exp(heights), dims[dim] // shards_of).reshape((-1,) + (1,) * (len(dims) - dim - 1))

    loudness = one(*pieces[0])
    for cut in pieces[1:]:
        loudness = loudness * one(*cut)
    return loudness


def scatter_about(own_key, extent, deviation, bound, split=(), kind=jnp.bfloat16):
    gain = shard_levels(own_key, extent, split, -0.22, 0.18) if split else 1.0
    entries = jax.random.normal(own_key, extent, jnp.float32) * deviation * gain
    return jnp.minimum(jnp.maximum(entries, -bound), bound).astype(kind)


def setup_inputs(seed: int = 0) -> dict:
    arg_keys = jax.random.split(jax.random.key(seed), 7)
    return {
        "features": scatter_about(arg_keys[0], (FRAMES, HEIGHT, CH, WIDTH), 1.0, 6.0, ((0, 4), (1, 8))),
        "block_shift": place_ends(jax.random.randint(arg_keys[1], (LEVELS, 4, FRAMES, HEIGHT // 8, WIDTH // 8), -SPAN, SPAN + 1), jax.random.fold_in(arg_keys[1], 1), -SPAN, SPAN).astype(jnp.int32),
        "quarter_pel": place_ends(jax.random.randint(arg_keys[2], (LEVELS, 4, FRAMES, HEIGHT // 8, WIDTH // 8), 0, 4), jax.random.fold_in(arg_keys[2], 1), 0, 3).astype(jnp.int32),
        "update_mask": place_ends((jax.random.randint(arg_keys[3], (LEVELS, FRAMES), 0, 4) < 3).astype(jnp.int32), jax.random.fold_in(arg_keys[3], 1), 0, 1),
        "uniting_weight": scatter_about(arg_keys[4], (3, 3, CH, 3 * CH), (27 * CH) ** -0.5, 0.15625),
        "mixing_weight": scatter_about(arg_keys[5], (3, 3, CH, CH), (9 * CH) ** -0.5, 0.25),
    }


def enlarge(values):
    return jnp.repeat(jnp.repeat(values, 8, axis=0), 8, axis=1)


def warp(panel_band, shifts, quarters):
    height, channels, columns = panel_band.shape
    margin = SPAN + 1
    padded = jnp.pad(panel_band.astype(jnp.float32), ((margin, margin), (0, 0), (margin, margin)))
    shift_rows = enlarge(shifts[0])
    shift_cols = enlarge(shifts[1])
    part_rows = enlarge(quarters[0]).astype(jnp.float32) * 0.25
    part_cols = enlarge(quarters[1]).astype(jnp.float32) * 0.25
    rows_at = jnp.arange(height, dtype=jnp.int32)[:, None] + shift_rows + margin
    cols_at = jnp.arange(columns, dtype=jnp.int32)[None, :] + shift_cols + margin
    summed = jnp.zeros((height, columns, channels), jnp.float32)
    for row_tap in (0, 1):
        weight_rows = part_rows if row_tap == 1 else 1.0 - part_rows
        for col_tap in (0, 1):
            weight_cols = part_cols if col_tap == 1 else 1.0 - part_cols
            picked = padded[rows_at + row_tap, :, cols_at + col_tap]
            summed = summed + (weight_rows * weight_cols)[:, :, None] * picked
    return jnp.transpose(summed, (0, 2, 1)).astype(jnp.bfloat16)


def convolve(inputs, weight):
    height, channels, columns = inputs.shape
    padded = jnp.pad(inputs.astype(jnp.float32), ((1, 1), (0, 0), (1, 1)))
    summed = jnp.zeros((height, weight.shape[2], columns), jnp.float32)
    for tap_row in range(3):
        for tap_col in range(3):
            window = padded[tap_row:tap_row + height, :, tap_col:tap_col + columns]
            summed = summed + jnp.einsum("oc,hcw->how", weight[tap_row, tap_col].astype(jnp.float32), window)
    return summed


def reference(features, block_shift, quarter_pel, update_mask, uniting_weight, mixing_weight):
    current = features
    for level_index in range(LEVELS - 1, -1, -1):
        distance = 2 ** level_index
        earlier = jnp.roll(current, distance, axis=0)
        following = jnp.roll(current, -distance, axis=0)
        shifts = jnp.moveaxis(block_shift[level_index], 1, 0)
        quarters = jnp.moveaxis(quarter_pel[level_index], 1, 0)
        masks = update_mask[level_index]

        def refine(item):
            before_band, after_band, own_band, shift_frame, quarter_frame, mask_value = item
            warped_earlier = warp(before_band, shift_frame[0:2], quarter_frame[0:2])
            warped_later = warp(after_band, shift_frame[2:4], quarter_frame[2:4])
            joined = jnp.concatenate([warped_earlier, warped_later, own_band], axis=1)
            uniting_sum = convolve(joined, uniting_weight)
            activation = (uniting_sum * jax.nn.sigmoid(uniting_sum)).astype(jnp.bfloat16)
            mixing_sum = convolve(activation, mixing_weight)
            return (own_band.astype(jnp.float32) + mask_value.astype(jnp.float32) * mixing_sum).astype(jnp.bfloat16)

        current = lax.map(refine, (earlier, following, current, shifts, quarters, masks))
    return current
```

```python
import functools

import jax
import jax.numpy as jnp
from jax import lax
from jax.experimental import pallas as pl
from jax.experimental.pallas import tpu as pltpu
from jax.sharding import PartitionSpec as P

LEVELS = 3
SPAN = 5
HALO = 8
REACH = 2
MESH = pl.DeviceIdType.MESH


def plan(frames):
    routes = {}
    for level in range(LEVELS):
        ahead = 2**level % frames
        behind = (frames - ahead) % frames
        if ahead == 0:
            routes[level] = ()
        elif ahead == behind:
            routes[level] = (ahead,)
        else:
            routes[level] = (ahead, behind)
    return routes


def kernel(frames, bands, features, grid_values, mask, uniting, mixing, out, *scratch):
    routes = plan(frames)
    total_refs = sum(len(routes[level]) for level in range(LEVELS))
    own = scratch[0]
    others = scratch[1]
    near, expanded, column_pass, joined, activation, w_unite, w_mix = scratch[2:9]
    send_own, recv_own, send_ref, recv_ref, send_near, recv_near = scratch[9:]
    local = features.shape[0]
    channels, columns = features.shape[1:]
    half = local // 2
    first = {}
    for level in range(LEVELS - 1, -1, -1):
        first[level] = sum(len(routes[k]) for k in range(level + 1, LEVELS))

    t = lax.axis_index("tm")
    r = lax.axis_index("rows")
    has_above = r > 0
    has_below = r < bands - 1
    up = (t, r - 1)
    down = (t, r + 1)
    hops = sorted({h for level in range(LEVELS) for h in routes[level]} | {frames - h for level in range(LEVELS) for h in routes[level]})

    barrier = pltpu.get_barrier_semaphore()

    @pl.when(has_above)
    def _():
        pl.semaphore_signal(barrier, inc=1, device_id=up, device_id_type=MESH)

    @pl.when(has_below)
    def _():
        pl.semaphore_signal(barrier, inc=1, device_id=down, device_id_type=MESH)

    for hop in hops:
        pl.semaphore_signal(barrier, inc=1, device_id=(lax.rem(t + hop, frames), r), device_id_type=MESH)

    zero_rows = jnp.zeros((HALO, channels, columns), jnp.bfloat16)

    @pl.when(jnp.logical_not(has_above))
    def _():
        for k in range(LEVELS):
            own[k, 0:HALO] = zero_rows
        for k in range(total_refs):
            others[k, 0:HALO] = zero_rows
        near[0] = jnp.zeros(near.shape[1:], near.dtype)

    @pl.when(jnp.logical_not(has_below))
    def _():
        for k in range(LEVELS):
            own[k, HALO + local : 2 * HALO + local] = zero_rows
        for k in range(total_refs):
            others[k, HALO + local : 2 * HALO + local] = zero_rows
        near[1] = jnp.zeros(near.shape[1:], near.dtype)

    own[LEVELS - 1, HALO : HALO + local] = features[...]

    pl.semaphore_wait(barrier, len(hops) + jnp.minimum(r, 1) + jnp.minimum(bands - 1 - r, 1))

    def remote(src, dst, send, recv, where):
        return pltpu.make_async_remote_copy(
            src_ref=src, dst_ref=dst, send_sem=send, recv_sem=recv, device_id=where, device_id_type=MESH
        )

    def near_copy(side):
        return remote(grid_values, near.at[side], send_near.at[side], recv_near.at[side], down if side == 0 else up)

    def own_copy(level, side):
        rows = REACH if routes[level] else HALO
        if side == 0:
            src, dst = HALO + local - rows, HALO - rows
        else:
            src, dst = HALO, HALO + local
        return remote(
            own.at[level, pl.ds(src, rows)],
            own.at[level, pl.ds(dst, rows)],
            send_own.at[level, side],
            recv_own.at[level, side],
            down if side == 0 else up,
        )

    def ref_copy(level, which, part):
        slot = first[level] + which
        rows = pl.ds(HALO + part * half, half)
        return remote(
            own.at[level, rows],
            others.at[slot, rows],
            send_ref.at[slot, part],
            recv_ref.at[slot, part],
            (lax.rem(t + routes[level][which], frames), r),
        )

    def edge_copy(level, which, side):
        slot = first[level] + which
        src, dst = (local, 0) if side == 0 else (HALO, HALO + local)
        return remote(
            others.at[slot, pl.ds(src, HALO)],
            others.at[slot, pl.ds(dst, HALO)],
            send_ref.at[slot, 2 + side],
            recv_ref.at[slot, 2 + side],
            down if side == 0 else up,
        )

    def when_sends(side):
        return has_below if side == 0 else has_above

    def when_gets(side):
        return has_above if side == 0 else has_below

    def start(copy, side):
        @pl.when(when_sends(side))
        def _():
            copy.start()

    def received(copy, side):
        @pl.when(when_gets(side))
        def _():
            copy.wait_recv()

    def sent(copy, side):
        @pl.when(when_sends(side))
        def _():
            copy.wait_send()

    def send_part(level, part):
        for which in range(len(routes[level])):
            ref_copy(level, which, part).start()
        start(own_copy(level, 1 - part), 1 - part)

    send_part(LEVELS - 1, 0)
    send_part(LEVELS - 1, 1)
    for side in (0, 1):
        start(near_copy(side), side)

    for tap in range(3):
        w_unite[:, tap * 3 * channels : (tap + 1) * 3 * channels] = uniting[tap].reshape(3 * channels, 3 * channels)
        w_mix[:, tap * channels : (tap + 1) * channels] = mixing[tap].reshape(3 * channels, channels)

    for side in (0, 1):
        received(near_copy(side), side)
    blocks = grid_values.shape[1]
    spread = (
        lax.broadcasted_iota(jnp.int32, (blocks, columns), 1) // 8
        == lax.broadcasted_iota(jnp.int32, (blocks, columns), 0)
    ).astype(jnp.bfloat16)
    for place, values in enumerate((near[0], grid_values[...], near[1])):
        expanded[place] = jnp.dot(values.astype(jnp.bfloat16), spread, preferred_element_type=jnp.float32)

    exists = (jnp.where(has_above, 1.0, 0.0), 1.0, 1.0, jnp.where(has_below, 1.0, 0.0))
    groups = ((-REACH, REACH, 0, 1), (0, 8, 1, 0), (8, 8, 1, 1), (local, REACH, 2, 0))
    quarters_at = grid_values.shape[0] // 2
    source_cols = lax.broadcasted_iota(jnp.int32, (columns, columns), 0).astype(jnp.float32)
    target_cols = lax.broadcasted_iota(jnp.int32, (1, columns), 1).astype(jnp.float32)

    def warp(level, component, source, to_channel):
        for group, (begin, rows, place, block_row) in enumerate(groups):
            y_at = (level * 4 + component) * 2 + block_row
            x_at = y_at + 2
            col_shift = expanded[place, x_at : x_at + 1, :]
            col_part = expanded[place, quarters_at + x_at : quarters_at + x_at + 1, :]
            col_pos = target_cols + col_shift + 0.25 * col_part
            hat = jnp.maximum(1.0 - jnp.abs(source_cols - col_pos), 0.0).astype(jnp.bfloat16)
            window = rows + 2 * SPAN + 1
            seen = source[pl.ds(HALO + begin - SPAN, window)].reshape(window * channels, columns)
            column_pass[0:window] = jnp.dot(seen, hat, preferred_element_type=jnp.float32).reshape(
                window, channels, columns
            )

            def piece(step, carry):
                lanes = pl.ds(pl.multiple_of((step // 4) * 128, 128), 128)
                chans = pl.ds(pl.multiple_of((step % 4) * 16, 16), 16)
                shift = jnp.broadcast_to(expanded[place, y_at : y_at + 1, lanes] + float(SPAN), (16, 128))
                part = jnp.broadcast_to(
                    0.25 * expanded[place, quarters_at + y_at : quarters_at + y_at + 1, lanes], (16, 128)
                )
                lines = [column_pass[i, chans, lanes] for i in range(window)]
                for size in (8, 4, 2, 1):
                    far = shift >= float(size)
                    shift = jnp.where(far, shift - float(size), shift)
                    keep = rows + size
                    lines = [
                        jnp.where(far, lines[i + size], lines[i]) if i + size < len(lines) else lines[i]
                        for i in range(keep)
                    ]
                for i in range(rows):
                    value = lines[i] + part * (lines[i + 1] - lines[i])
                    if group in (0, 3):
                        value = value * exists[group]
                    to = pl.ds(pl.multiple_of(to_channel + (step % 4) * 16, 16), 16)
                    joined[begin + REACH + i, to, lanes] = value.astype(jnp.bfloat16)
                return carry

            lax.fori_loop(0, (channels // 16) * (columns // 128), piece, 0)

    lane = lax.broadcasted_iota(jnp.int32, (channels, columns), 1)
    not_first = lane > 0
    not_last = lane < columns - 1

    def taps(product):
        left, middle, right = (product[i * channels : (i + 1) * channels] for i in range(3))
        return (
            middle
            + jnp.where(not_first, pltpu.roll(left, 1, 1), 0.0)
            + jnp.where(not_last, pltpu.roll(right, columns - 1, 1), 0.0)
        )

    def unite(begin, end):
        def row(y, carry):
            slab = joined[pl.ds(y, 3)].reshape(9 * channels, columns)
            total = taps(jnp.dot(w_unite[...], slab, preferred_element_type=jnp.float32))
            activation[y] = (total * jax.nn.sigmoid(total)).astype(jnp.bfloat16)
            return carry

        lax.fori_loop(begin, end, row, 0)

    def mix(level, begin, end):
        kept = mask[level, 0].astype(jnp.float32)

        def row(y, carry):
            slab = activation[pl.ds(y, 3)].reshape(3 * channels, columns)
            total = taps(jnp.dot(w_mix[...], slab, preferred_element_type=jnp.float32))
            fresh = (own[level, HALO + y].astype(jnp.float32) + kept * total).astype(jnp.bfloat16)
            if level > 0:
                own[level - 1, HALO + y] = fresh
            else:
                out[y] = fresh
            return carry

        lax.fori_loop(begin, end, row, 0)

    for level in range(LEVELS - 1, -1, -1):
        count = len(routes[level])
        for side in (1, 0):
            received(own_copy(level, side), side)
        joined[:, 2 * channels : 3 * channels, :] = own[level, pl.ds(HALO - REACH, local + 2 * REACH)]
        for part in (0, 1):
            for which in range(count):
                ref_copy(level, which, part).wait_recv()
                start(edge_copy(level, which, 1 - part), 1 - part)
        for which in range(2):
            if which < count:
                for side in (1, 0):
                    received(edge_copy(level, which, side), side)
            source = others.at[first[level] + min(which, count - 1)] if count else own.at[level]
            warp(level, 2 * which, source, which * channels)
        unite(0, half + 2)

        @pl.when(jnp.logical_not(has_above))
        def _():
            activation[0] = jnp.zeros((channels, columns), jnp.bfloat16)

        mix(level, 0, half)
        if level > 0:
            send_part(level - 1, 0)
        unite(half + 2, local + 2)

        @pl.when(jnp.logical_not(has_below))
        def _():
            activation[local + 1] = jnp.zeros((channels, columns), jnp.bfloat16)

        mix(level, half, local)
        if level > 0:
            send_part(level - 1, 1)

    for side in (0, 1):
        sent(near_copy(side), side)
        for level in range(LEVELS):
            sent(own_copy(level, side), side)
            for which in range(len(routes[level])):
                ref_copy(level, which, side).wait_send()
                sent(edge_copy(level, which, side), side)


def shards(frames, bands, features, block_shift, quarter_pel, update_mask, uniting_weight, mixing_weight):
    band = features[0]
    local, channels, columns = band.shape
    blocks = block_shift.shape[-1]
    grid_values = jnp.concatenate(
        [block_shift.reshape(-1, blocks), quarter_pel.reshape(-1, blocks)], axis=0
    ).astype(jnp.float32)
    total_refs = max(1, sum(len(route) for route in plan(frames).values()))
    vmem = pl.BlockSpec(memory_space=pltpu.VMEM)
    dma = pltpu.SemaphoreType.DMA
    refined = pl.pallas_call(
        functools.partial(kernel, frames, bands),
        out_shape=jax.ShapeDtypeStruct(band.shape, jnp.bfloat16),
        in_specs=[vmem, vmem, pl.BlockSpec(memory_space=pltpu.SMEM), vmem, vmem],
        out_specs=vmem,
        scratch_shapes=[
            pltpu.VMEM((LEVELS, local + 2 * HALO, channels, columns), jnp.bfloat16),
            pltpu.VMEM((total_refs, local + 2 * HALO, channels, columns), jnp.bfloat16),
            pltpu.VMEM((2,) + grid_values.shape, jnp.float32),
            pltpu.VMEM((3, grid_values.shape[0], columns), jnp.float32),
            pltpu.VMEM((8 + 2 * SPAN + 1, channels, columns), jnp.float32),
            pltpu.VMEM((local + 2 * REACH, 3 * channels, columns), jnp.bfloat16),
            pltpu.VMEM((local + 2, channels, columns), jnp.bfloat16),
            pltpu.VMEM((3 * channels, 9 * channels), jnp.bfloat16),
            pltpu.VMEM((3 * channels, 3 * channels), jnp.bfloat16),
            dma((LEVELS, 2)),
            dma((LEVELS, 2)),
            dma((total_refs, 4)),
            dma((total_refs, 4)),
            dma((2,)),
            dma((2,)),
        ],
        compiler_params=pltpu.CompilerParams(
            collective_id=0, has_side_effects=True, vmem_limit_bytes=40 * 1024 * 1024
        ),
    )(band, grid_values, update_mask, uniting_weight, mixing_weight)
    return refined[None]


def solution(mesh):
    placed = (
        P("tm", "rows", None, None),
        P(None, None, "tm", "rows", None),
        P(None, None, "tm", "rows", None),
        P(None, "tm"),
        P(),
        P(),
    )
    return jax.shard_map(
        functools.partial(shards, mesh.shape["tm"], mesh.shape["rows"]),
        mesh=mesh,
        in_specs=placed,
        out_specs=P("tm", "rows", None, None),
        check_vma=False,
    )
```

```python
import functools

import jax
import jax.numpy as jnp
from jax import lax
from jax.experimental import pallas as pl
from jax.experimental.pallas import tpu as pltpu
from jax.sharding import PartitionSpec as P

LEVELS = 3
SPAN = 5
HALO = 8
REACH = 2
MESH = pl.DeviceIdType.MESH


def plan(frames):
    routes = {}
    for level in range(LEVELS):
        ahead = 2**level % frames
        behind = (frames - ahead) % frames
        if ahead == 0:
            routes[level] = ()
        elif ahead == behind:
            routes[level] = (ahead,)
        else:
            routes[level] = (ahead, behind)
    return routes


def kernel(frames, bands, features, grid_values, mask, uniting, mixing, out, *scratch):
    routes = plan(frames)
    total_refs = sum(len(routes[level]) for level in range(LEVELS))
    own = scratch[0]
    others = scratch[1]
    near, expanded, column_pass, joined, activation, w_unite, w_mix, uniting_here, mixing_here, fetched = scratch[2:12]
    send_own, recv_own, send_ref, recv_ref, send_near, recv_near = scratch[12:]
    local = features.shape[0]
    channels, columns = features.shape[1:]
    half = local // 2
    first = {}
    for level in range(LEVELS - 1, -1, -1):
        first[level] = sum(len(routes[k]) for k in range(level + 1, LEVELS))

    t = lax.axis_index("tm")
    r = lax.axis_index("rows")
    has_above = r > 0
    has_below = r < bands - 1
    up = (t, r - 1)
    down = (t, r + 1)
    hops = sorted({h for level in range(LEVELS) for h in routes[level]} | {frames - h for level in range(LEVELS) for h in routes[level]})

    band_copy = pltpu.make_async_copy(features, own.at[LEVELS - 1, pl.ds(HALO, local)], fetched.at[0])
    weight_copies = (
        pltpu.make_async_copy(uniting, uniting_here, fetched.at[1]),
        pltpu.make_async_copy(mixing, mixing_here, fetched.at[2]),
    )
    band_copy.start()
    for copy in weight_copies:
        copy.start()

    barrier = pltpu.get_barrier_semaphore()

    @pl.when(has_above)
    def _():
        pl.semaphore_signal(barrier, inc=1, device_id=up, device_id_type=MESH)

    @pl.when(has_below)
    def _():
        pl.semaphore_signal(barrier, inc=1, device_id=down, device_id_type=MESH)

    for hop in hops:
        pl.semaphore_signal(barrier, inc=1, device_id=(lax.rem(t + hop, frames), r), device_id_type=MESH)

    zero_rows = jnp.zeros((HALO, channels, columns), jnp.bfloat16)

    @pl.when(jnp.logical_not(has_above))
    def _():
        for k in range(LEVELS):
            own[k, 0:HALO] = zero_rows
        for k in range(total_refs):
            others[k, 0:HALO] = zero_rows
        near[0] = jnp.zeros(near.shape[1:], near.dtype)

    @pl.when(jnp.logical_not(has_below))
    def _():
        for k in range(LEVELS):
            own[k, HALO + local : 2 * HALO + local] = zero_rows
        for k in range(total_refs):
            others[k, HALO + local : 2 * HALO + local] = zero_rows
        near[1] = jnp.zeros(near.shape[1:], near.dtype)


    pl.semaphore_wait(barrier, len(hops) + jnp.minimum(r, 1) + jnp.minimum(bands - 1 - r, 1))

    def remote(src, dst, send, recv, where):
        return pltpu.make_async_remote_copy(
            src_ref=src, dst_ref=dst, send_sem=send, recv_sem=recv, device_id=where, device_id_type=MESH
        )

    def near_copy(side):
        return remote(grid_values, near.at[side], send_near.at[side], recv_near.at[side], down if side == 0 else up)

    def own_copy(level, side):
        rows = REACH if routes[level] else HALO
        if side == 0:
            src, dst = HALO + local - rows, HALO - rows
        else:
            src, dst = HALO, HALO + local
        return remote(
            own.at[level, pl.ds(src, rows)],
            own.at[level, pl.ds(dst, rows)],
            send_own.at[level, side],
            recv_own.at[level, side],
            down if side == 0 else up,
        )

    def ref_copy(level, which, part):
        slot = first[level] + which
        rows = pl.ds(HALO + part * half, half)
        return remote(
            own.at[level, rows],
            others.at[slot, rows],
            send_ref.at[slot, part],
            recv_ref.at[slot, part],
            (lax.rem(t + routes[level][which], frames), r),
        )

    def edge_copy(level, which, side):
        slot = first[level] + which
        src, dst = (local, 0) if side == 0 else (HALO, HALO + local)
        return remote(
            others.at[slot, pl.ds(src, HALO)],
            others.at[slot, pl.ds(dst, HALO)],
            send_ref.at[slot, 2 + side],
            recv_ref.at[slot, 2 + side],
            down if side == 0 else up,
        )

    def when_sends(side):
        return has_below if side == 0 else has_above

    def when_gets(side):
        return has_above if side == 0 else has_below

    def start(copy, side):
        @pl.when(when_sends(side))
        def _():
            copy.start()

    def received(copy, side):
        @pl.when(when_gets(side))
        def _():
            copy.wait_recv()

    def sent(copy, side):
        @pl.when(when_sends(side))
        def _():
            copy.wait_send()

    def send_part(level, part):
        for which in range(len(routes[level])):
            ref_copy(level, which, part).start()
        start(own_copy(level, 1 - part), 1 - part)

    band_copy.wait()
    send_part(LEVELS - 1, 0)
    send_part(LEVELS - 1, 1)
    for side in (0, 1):
        start(near_copy(side), side)

    tall = 3 * channels
    w_unite[...] = jnp.zeros_like(w_unite)
    w_mix[...] = jnp.zeros_like(w_mix)
    for copy in weight_copies:
        copy.wait()
    for pair in range(2):
        for tap in range(3):
            at = pair + tap
            w_unite[pair * tall : (pair + 1) * tall, at * tall : (at + 1) * tall] = uniting_here[tap].reshape(tall, tall)
            w_mix[pair * tall : (pair + 1) * tall, at * channels : (at + 1) * channels] = mixing_here[tap].reshape(
                tall, channels
            )

    for side in (0, 1):
        received(near_copy(side), side)
    blocks = grid_values.shape[1]
    spread = (
        lax.broadcasted_iota(jnp.int32, (blocks, columns), 1) // 8
        == lax.broadcasted_iota(jnp.int32, (blocks, columns), 0)
    ).astype(jnp.bfloat16)
    for place, values in enumerate((near[0], grid_values[...], near[1])):
        expanded[place] = jnp.dot(values.astype(jnp.bfloat16), spread, preferred_element_type=jnp.float32)

    exists = (jnp.where(has_above, 1.0, 0.0), 1.0, 1.0, jnp.where(has_below, 1.0, 0.0))
    groups = ((-REACH, REACH, 0, 1), (0, 8, 1, 0), (8, 8, 1, 1), (local, REACH, 2, 0))
    quarters_at = grid_values.shape[0] // 2
    source_cols = lax.broadcasted_iota(jnp.int32, (columns, columns), 0).astype(jnp.float32)
    target_cols = lax.broadcasted_iota(jnp.int32, (1, columns), 1).astype(jnp.float32)

    def warp(level, component, source, to_channel):
        for group, (begin, rows, place, block_row) in enumerate(groups):
            y_at = (level * 4 + component) * 2 + block_row
            x_at = y_at + 2
            col_shift = expanded[place, x_at : x_at + 1, :]
            col_part = expanded[place, quarters_at + x_at : quarters_at + x_at + 1, :]
            col_pos = target_cols + col_shift + 0.25 * col_part
            hat = jnp.maximum(1.0 - jnp.abs(source_cols - col_pos), 0.0).astype(jnp.bfloat16)
            window = rows + 2 * SPAN + 1
            seen = source[pl.ds(HALO + begin - SPAN, window)].reshape(window * channels, columns)
            column_pass[0:window] = jnp.dot(seen, hat, preferred_element_type=jnp.float32).reshape(
                window, channels, columns
            )

            def piece(step, carry):
                lanes = pl.ds(pl.multiple_of((step // 4) * 128, 128), 128)
                chans = pl.ds(pl.multiple_of((step % 4) * 16, 16), 16)
                shift = jnp.broadcast_to(expanded[place, y_at : y_at + 1, lanes] + float(SPAN), (16, 128))
                part = jnp.broadcast_to(
                    0.25 * expanded[place, quarters_at + y_at : quarters_at + y_at + 1, lanes], (16, 128)
                )
                lines = [column_pass[i, chans, lanes] for i in range(window)]
                for size in (8, 4, 2, 1):
                    far = shift >= float(size)
                    shift = jnp.where(far, shift - float(size), shift)
                    keep = rows + size
                    lines = [
                        jnp.where(far, lines[i + size], lines[i]) if i + size < len(lines) else lines[i]
                        for i in range(keep)
                    ]
                for i in range(rows):
                    value = lines[i] + part * (lines[i + 1] - lines[i])
                    if group in (0, 3):
                        value = value * exists[group]
                    to = pl.ds(pl.multiple_of(to_channel + (step % 4) * 16, 16), 16)
                    joined[begin + REACH + i, to, lanes] = value.astype(jnp.bfloat16)
                return carry

            lax.fori_loop(0, (channels // 16) * (columns // 128), piece, 0, unroll=4)

    lane = lax.broadcasted_iota(jnp.int32, (channels, columns), 1)
    not_first = lane > 0
    not_last = lane < columns - 1

    def taps(product):
        left, middle, right = (product[i * channels : (i + 1) * channels] for i in range(3))
        return (
            middle
            + jnp.where(not_first, pltpu.roll(left, 1, 1), 0.0)
            + jnp.where(not_last, pltpu.roll(right, columns - 1, 1), 0.0)
        )

    def unite(begin, end):
        def rows(step, carry):
            y = begin + 2 * step
            slab = joined[pl.ds(y, 4)].reshape(12 * channels, columns)
            product = jnp.dot(w_unite[...], slab, preferred_element_type=jnp.float32)
            for pair in range(2):
                total = taps(product[pair * tall : (pair + 1) * tall])
                activation[y + pair] = (total * jax.nn.sigmoid(total)).astype(jnp.bfloat16)
            return carry

        lax.fori_loop(0, (end - begin) // 2, rows, 0, unroll=True)

    def mix(level, begin, end):
        kept = mask[level, 0].astype(jnp.float32)

        def rows(step, carry):
            y = begin + 2 * step
            slab = activation[pl.ds(y, 4)].reshape(4 * channels, columns)
            product = jnp.dot(w_mix[...], slab, preferred_element_type=jnp.float32)
            for pair in range(2):
                total = taps(product[pair * tall : (pair + 1) * tall])
                fresh = (own[level, HALO + y + pair].astype(jnp.float32) + kept * total).astype(jnp.bfloat16)
                if level > 0:
                    own[level - 1, HALO + y + pair] = fresh
                else:
                    out[y + pair] = fresh
            return carry

        lax.fori_loop(0, (end - begin) // 2, rows, 0, unroll=True)

    for level in range(LEVELS - 1, -1, -1):
        count = len(routes[level])
        for side in (1, 0):
            received(own_copy(level, side), side)
        joined[:, 2 * channels : 3 * channels, :] = own[level, pl.ds(HALO - REACH, local + 2 * REACH)]
        for part in (0, 1):
            for which in range(count):
                ref_copy(level, which, part).wait_recv()
                start(edge_copy(level, which, 1 - part), 1 - part)
        for which in range(2):
            if which < count:
                for side in (1, 0):
                    received(edge_copy(level, which, side), side)
            source = others.at[first[level] + min(which, count - 1)] if count else own.at[level]
            warp(level, 2 * which, source, which * channels)
        unite(0, half + 2)

        @pl.when(jnp.logical_not(has_above))
        def _():
            activation[0] = jnp.zeros((channels, columns), jnp.bfloat16)

        mix(level, 0, half)
        if level > 0:
            send_part(level - 1, 0)
        unite(half + 2, local + 2)

        @pl.when(jnp.logical_not(has_below))
        def _():
            activation[local + 1] = jnp.zeros((channels, columns), jnp.bfloat16)

        mix(level, half, local)
        if level > 0:
            send_part(level - 1, 1)

    for side in (0, 1):
        sent(near_copy(side), side)
        for level in range(LEVELS):
            sent(own_copy(level, side), side)
            for which in range(len(routes[level])):
                ref_copy(level, which, side).wait_send()
                sent(edge_copy(level, which, side), side)


def shards(frames, bands, features, block_shift, quarter_pel, update_mask, uniting_weight, mixing_weight):
    band = features[0]
    local, channels, columns = band.shape
    blocks = block_shift.shape[-1]
    grid_values = jnp.concatenate(
        [block_shift.reshape(-1, blocks), quarter_pel.reshape(-1, blocks)], axis=0
    ).astype(jnp.float32)
    total_refs = max(1, sum(len(route) for route in plan(frames).values()))
    vmem = pl.BlockSpec(memory_space=pltpu.VMEM)
    anywhere = pl.BlockSpec(memory_space=pl.ANY)
    dma = pltpu.SemaphoreType.DMA
    refined = pl.pallas_call(
        functools.partial(kernel, frames, bands),
        out_shape=jax.ShapeDtypeStruct(band.shape, jnp.bfloat16),
        in_specs=[anywhere, vmem, pl.BlockSpec(memory_space=pltpu.SMEM), anywhere, anywhere],
        out_specs=vmem,
        scratch_shapes=[
            pltpu.VMEM((LEVELS, local + 2 * HALO, channels, columns), jnp.bfloat16),
            pltpu.VMEM((total_refs, local + 2 * HALO, channels, columns), jnp.bfloat16),
            pltpu.VMEM((2,) + grid_values.shape, jnp.float32),
            pltpu.VMEM((3, grid_values.shape[0], columns), jnp.float32),
            pltpu.VMEM((8 + 2 * SPAN + 1, channels, columns), jnp.float32),
            pltpu.VMEM((local + 2 * REACH, 3 * channels, columns), jnp.bfloat16),
            pltpu.VMEM((local + 2, channels, columns), jnp.bfloat16),
            pltpu.VMEM((6 * channels, 12 * channels), jnp.bfloat16),
            pltpu.VMEM((6 * channels, 4 * channels), jnp.bfloat16),
            pltpu.VMEM(uniting_weight.shape, jnp.bfloat16),
            pltpu.VMEM(mixing_weight.shape, jnp.bfloat16),
            dma((3,)),
            dma((LEVELS, 2)),
            dma((LEVELS, 2)),
            dma((total_refs, 4)),
            dma((total_refs, 4)),
            dma((2,)),
            dma((2,)),
        ],
        compiler_params=pltpu.CompilerParams(
            collective_id=0, has_side_effects=True, vmem_limit_bytes=40 * 1024 * 1024
        ),
    )(band, grid_values, update_mask, uniting_weight, mixing_weight)
    return refined[None]


def solution(mesh):
    placed = (
        P("tm", "rows", None, None),
        P(None, None, "tm", "rows", None),
        P(None, None, "tm", "rows", None),
        P(None, "tm"),
        P(),
        P(),
    )
    return jax.shard_map(
        functools.partial(shards, mesh.shape["tm"], mesh.shape["rows"]),
        mesh=mesh,
        in_specs=placed,
        out_specs=P("tm", "rows", None, None),
        check_vma=False,
    )
```

```python
import functools

import jax
import jax.numpy as jnp
from jax import lax
from jax.experimental import pallas as pl
from jax.experimental.pallas import tpu as pltpu
from jax.sharding import PartitionSpec as P

LEVELS = 3
SPAN = 5
HALO = 8
PARTS = 4
REACH = 2
MESH = pl.DeviceIdType.MESH


def plan(frames):
    routes = {}
    for level in range(LEVELS):
        ahead = 2**level % frames
        behind = (frames - ahead) % frames
        if ahead == 0:
            routes[level] = ()
        elif ahead == behind:
            routes[level] = (ahead,)
        else:
            routes[level] = (ahead, behind)
    return routes


def kernel(frames, bands, features, grid_values, mask, uniting, mixing, out, *scratch):
    routes = plan(frames)
    total_refs = sum(len(routes[level]) for level in range(LEVELS))
    own = scratch[0]
    others = scratch[1]
    near, expanded, column_pass, joined, activation, w_unite, w_mix, uniting_here, mixing_here, fetched = scratch[2:12]
    send_own, recv_own, send_ref, recv_ref, send_near, recv_near = scratch[12:]
    local = features.shape[0]
    channels, columns = features.shape[1:]
    size_of_part = local // PARTS
    first = {}
    for level in range(LEVELS - 1, -1, -1):
        first[level] = sum(len(routes[k]) for k in range(level + 1, LEVELS))

    t = lax.axis_index("tm")
    r = lax.axis_index("rows")
    has_above = r > 0
    has_below = r < bands - 1
    up = (t, r - 1)
    down = (t, r + 1)
    hops = sorted({h for level in range(LEVELS) for h in routes[level]} | {frames - h for level in range(LEVELS) for h in routes[level]})

    band_copy = pltpu.make_async_copy(features, own.at[LEVELS - 1, pl.ds(HALO, local)], fetched.at[0])
    weight_copies = (
        pltpu.make_async_copy(uniting, uniting_here, fetched.at[1]),
        pltpu.make_async_copy(mixing, mixing_here, fetched.at[2]),
    )
    band_copy.start()
    for copy in weight_copies:
        copy.start()

    barrier = pltpu.get_barrier_semaphore()

    @pl.when(has_above)
    def _():
        pl.semaphore_signal(barrier, inc=1, device_id=up, device_id_type=MESH)

    @pl.when(has_below)
    def _():
        pl.semaphore_signal(barrier, inc=1, device_id=down, device_id_type=MESH)

    for hop in hops:
        pl.semaphore_signal(barrier, inc=1, device_id=(lax.rem(t + hop, frames), r), device_id_type=MESH)

    zero_rows = jnp.zeros((HALO, channels, columns), jnp.bfloat16)

    @pl.when(jnp.logical_not(has_above))
    def _():
        for k in range(LEVELS):
            own[k, 0:HALO] = zero_rows
        for k in range(total_refs):
            others[k, 0:HALO] = zero_rows
        near[0] = jnp.zeros(near.shape[1:], near.dtype)

    @pl.when(jnp.logical_not(has_below))
    def _():
        for k in range(LEVELS):
            own[k, HALO + local : 2 * HALO + local] = zero_rows
        for k in range(total_refs):
            others[k, HALO + local : 2 * HALO + local] = zero_rows
        near[1] = jnp.zeros(near.shape[1:], near.dtype)


    pl.semaphore_wait(barrier, len(hops) + jnp.minimum(r, 1) + jnp.minimum(bands - 1 - r, 1))

    def remote(src, dst, send, recv, where):
        return pltpu.make_async_remote_copy(
            src_ref=src, dst_ref=dst, send_sem=send, recv_sem=recv, device_id=where, device_id_type=MESH
        )

    def near_copy(side):
        return remote(grid_values, near.at[side], send_near.at[side], recv_near.at[side], down if side == 0 else up)

    def own_copy(level, side):
        rows = REACH if routes[level] else HALO
        if side == 0:
            src, dst = HALO + local - rows, HALO - rows
        else:
            src, dst = HALO, HALO + local
        return remote(
            own.at[level, pl.ds(src, rows)],
            own.at[level, pl.ds(dst, rows)],
            send_own.at[level, side],
            recv_own.at[level, side],
            down if side == 0 else up,
        )

    def ref_copy(level, which, part):
        slot = first[level] + which
        rows = pl.ds(HALO + part * size_of_part, size_of_part)
        return remote(
            own.at[level, rows],
            others.at[slot, rows],
            send_ref.at[slot, part],
            recv_ref.at[slot, part],
            (lax.rem(t + routes[level][which], frames), r),
        )

    def edge_side(part):
        return 1 if part < PARTS // 2 else 0

    def edge_copy(level, which, part):
        slot = first[level] + which
        side = edge_side(part)
        src = HALO + part * size_of_part
        dst = src + local if side == 1 else src - local
        return remote(
            others.at[slot, pl.ds(src, size_of_part)],
            others.at[slot, pl.ds(dst, size_of_part)],
            send_ref.at[slot, PARTS + part],
            recv_ref.at[slot, PARTS + part],
            down if side == 0 else up,
        )

    def when_sends(side):
        return has_below if side == 0 else has_above

    def when_gets(side):
        return has_above if side == 0 else has_below

    def start(copy, side):
        @pl.when(when_sends(side))
        def _():
            copy.start()

    def received(copy, side):
        @pl.when(when_gets(side))
        def _():
            copy.wait_recv()

    def sent(copy, side):
        @pl.when(when_sends(side))
        def _():
            copy.wait_send()

    def send_part(level, part):
        for which in range(len(routes[level])):
            ref_copy(level, which, part).start()
        if part == (0 if routes[level] else PARTS // 2 - 1):
            start(own_copy(level, 1), 1)
        if part == PARTS - 1:
            start(own_copy(level, 0), 0)

    band_copy.wait()
    for part in range(PARTS):
        send_part(LEVELS - 1, part)
    for side in (0, 1):
        start(near_copy(side), side)

    tall = 3 * channels
    w_unite[...] = jnp.zeros_like(w_unite)
    w_mix[...] = jnp.zeros_like(w_mix)
    for copy in weight_copies:
        copy.wait()
    for pair in range(2):
        for tap in range(3):
            at = pair + tap
            w_unite[pair * tall : (pair + 1) * tall, at * tall : (at + 1) * tall] = uniting_here[tap].reshape(tall, tall)
            w_mix[pair * tall : (pair + 1) * tall, at * channels : (at + 1) * channels] = mixing_here[tap].reshape(
                tall, channels
            )

    for side in (0, 1):
        received(near_copy(side), side)
    blocks = grid_values.shape[1]
    spread = (
        lax.broadcasted_iota(jnp.int32, (blocks, columns), 1) // 8
        == lax.broadcasted_iota(jnp.int32, (blocks, columns), 0)
    ).astype(jnp.bfloat16)
    for place, values in enumerate((near[0], grid_values[...], near[1])):
        expanded[place] = jnp.dot(values.astype(jnp.bfloat16), spread, preferred_element_type=jnp.float32)

    exists = (jnp.where(has_above, 1.0, 0.0), 1.0, 1.0, jnp.where(has_below, 1.0, 0.0))
    groups = ((-REACH, REACH, 0, 1), (0, 8, 1, 0), (8, 8, 1, 1), (local, REACH, 2, 0))
    quarters_at = grid_values.shape[0] // 2
    source_cols = lax.broadcasted_iota(jnp.int32, (columns, columns), 0).astype(jnp.float32)
    target_cols = lax.broadcasted_iota(jnp.int32, (1, columns), 1).astype(jnp.float32)

    def warp(level, component, source, to_channel):
        for group, (begin, rows, place, block_row) in enumerate(groups):
            y_at = (level * 4 + component) * 2 + block_row
            x_at = y_at + 2
            col_shift = expanded[place, x_at : x_at + 1, :]
            col_part = expanded[place, quarters_at + x_at : quarters_at + x_at + 1, :]
            col_pos = target_cols + col_shift + 0.25 * col_part
            hat = jnp.maximum(1.0 - jnp.abs(source_cols - col_pos), 0.0).astype(jnp.bfloat16)
            window = rows + 2 * SPAN + 1
            seen = source[pl.ds(HALO + begin - SPAN, window)].reshape(window * channels, columns)
            column_pass[0:window] = jnp.dot(seen, hat, preferred_element_type=jnp.float32).reshape(
                window, channels, columns
            )

            def piece(step, carry):
                lanes = pl.ds(pl.multiple_of((step // 4) * 128, 128), 128)
                chans = pl.ds(pl.multiple_of((step % 4) * 16, 16), 16)
                shift = jnp.broadcast_to(expanded[place, y_at : y_at + 1, lanes] + float(SPAN), (16, 128))
                part = jnp.broadcast_to(
                    0.25 * expanded[place, quarters_at + y_at : quarters_at + y_at + 1, lanes], (16, 128)
                )
                lines = [column_pass[i, chans, lanes] for i in range(window)]
                for size in (8, 4, 2, 1):
                    far = shift >= float(size)
                    shift = jnp.where(far, shift - float(size), shift)
                    keep = rows + size
                    lines = [
                        jnp.where(far, lines[i + size], lines[i]) if i + size < len(lines) else lines[i]
                        for i in range(keep)
                    ]
                for i in range(rows):
                    value = lines[i] + part * (lines[i + 1] - lines[i])
                    if group in (0, 3):
                        value = value * exists[group]
                    to = pl.ds(pl.multiple_of(to_channel + (step % 4) * 16, 16), 16)
                    joined[begin + REACH + i, to, lanes] = value.astype(jnp.bfloat16)
                return carry

            lax.fori_loop(0, (channels // 16) * (columns // 128), piece, 0, unroll=4)

    lane = lax.broadcasted_iota(jnp.int32, (channels, columns), 1)
    not_first = lane > 0
    not_last = lane < columns - 1

    def taps(product):
        left, middle, right = (product[i * channels : (i + 1) * channels] for i in range(3))
        return (
            middle
            + jnp.where(not_first, pltpu.roll(left, 1, 1), 0.0)
            + jnp.where(not_last, pltpu.roll(right, columns - 1, 1), 0.0)
        )

    def unite(begin, end):
        def rows(step, carry):
            y = begin + 2 * step
            slab = joined[pl.ds(y, 4)].reshape(12 * channels, columns)
            product = jnp.dot(w_unite[...], slab, preferred_element_type=jnp.float32)
            for pair in range(2):
                total = taps(product[pair * tall : (pair + 1) * tall])
                activation[y + pair] = (total * jax.nn.sigmoid(total)).astype(jnp.bfloat16)
            return carry

        lax.fori_loop(0, (end - begin) // 2, rows, 0, unroll=True)

    def mix(level, begin, end):
        kept = mask[level, 0].astype(jnp.float32)

        def rows(step, carry):
            y = begin + 2 * step
            slab = activation[pl.ds(y, 4)].reshape(4 * channels, columns)
            product = jnp.dot(w_mix[...], slab, preferred_element_type=jnp.float32)
            for pair in range(2):
                total = taps(product[pair * tall : (pair + 1) * tall])
                fresh = (own[level, HALO + y + pair].astype(jnp.float32) + kept * total).astype(jnp.bfloat16)
                if level > 0:
                    own[level - 1, HALO + y + pair] = fresh
                else:
                    out[y + pair] = fresh
            return carry

        lax.fori_loop(0, (end - begin) // 2, rows, 0, unroll=True)

    for level in range(LEVELS - 1, -1, -1):
        count = len(routes[level])
        for side in (1, 0):
            received(own_copy(level, side), side)
        joined[:, 2 * channels : 3 * channels, :] = own[level, pl.ds(HALO - REACH, local + 2 * REACH)]
        for part in range(PARTS):
            for which in range(count):
                ref_copy(level, which, part).wait_recv()
                start(edge_copy(level, which, part), edge_side(part))
        for which in range(2):
            if which < count:
                for part in range(PARTS):
                    received(edge_copy(level, which, part), edge_side(part))
            source = others.at[first[level] + min(which, count - 1)] if count else own.at[level]
            warp(level, 2 * which, source, which * channels)
        for part in range(PARTS):
            begin, end = part * size_of_part, (part + 1) * size_of_part
            unite(begin + 2 if part else 0, end + 2)
            if part == 0:

                @pl.when(jnp.logical_not(has_above))
                def _():
                    activation[0] = jnp.zeros((channels, columns), jnp.bfloat16)

            if part == PARTS - 1:

                @pl.when(jnp.logical_not(has_below))
                def _():
                    activation[local + 1] = jnp.zeros((channels, columns), jnp.bfloat16)

            mix(level, begin, end)
            if level > 0:
                send_part(level - 1, part)

    for side in (0, 1):
        sent(near_copy(side), side)
        for level in range(LEVELS):
            sent(own_copy(level, side), side)
    for level in range(LEVELS):
        for which in range(len(routes[level])):
            for part in range(PARTS):
                ref_copy(level, which, part).wait_send()
                sent(edge_copy(level, which, part), edge_side(part))


def shards(frames, bands, features, block_shift, quarter_pel, update_mask, uniting_weight, mixing_weight):
    band = features[0]
    local, channels, columns = band.shape
    blocks = block_shift.shape[-1]
    grid_values = jnp.concatenate(
        [block_shift.reshape(-1, blocks), quarter_pel.reshape(-1, blocks)], axis=0
    ).astype(jnp.float32)
    total_refs = max(1, sum(len(route) for route in plan(frames).values()))
    vmem = pl.BlockSpec(memory_space=pltpu.VMEM)
    anywhere = pl.BlockSpec(memory_space=pl.ANY)
    dma = pltpu.SemaphoreType.DMA
    refined = pl.pallas_call(
        functools.partial(kernel, frames, bands),
        out_shape=jax.ShapeDtypeStruct(band.shape, jnp.bfloat16),
        in_specs=[anywhere, vmem, pl.BlockSpec(memory_space=pltpu.SMEM), anywhere, anywhere],
        out_specs=vmem,
        scratch_shapes=[
            pltpu.VMEM((LEVELS, local + 2 * HALO, channels, columns), jnp.bfloat16),
            pltpu.VMEM((total_refs, local + 2 * HALO, channels, columns), jnp.bfloat16),
            pltpu.VMEM((2,) + grid_values.shape, jnp.float32),
            pltpu.VMEM((3, grid_values.shape[0], columns), jnp.float32),
            pltpu.VMEM((8 + 2 * SPAN + 1, channels, columns), jnp.float32),
            pltpu.VMEM((local + 2 * REACH, 3 * channels, columns), jnp.bfloat16),
            pltpu.VMEM((local + 2, channels, columns), jnp.bfloat16),
            pltpu.VMEM((6 * channels, 12 * channels), jnp.bfloat16),
            pltpu.VMEM((6 * channels, 4 * channels), jnp.bfloat16),
            pltpu.VMEM(uniting_weight.shape, jnp.bfloat16),
            pltpu.VMEM(mixing_weight.shape, jnp.bfloat16),
            dma((3,)),
            dma((LEVELS, 2)),
            dma((LEVELS, 2)),
            dma((total_refs, 2 * PARTS)),
            dma((total_refs, 2 * PARTS)),
            dma((2,)),
            dma((2,)),
        ],
        compiler_params=pltpu.CompilerParams(
            collective_id=0, has_side_effects=True, vmem_limit_bytes=40 * 1024 * 1024
        ),
    )(band, grid_values, update_mask, uniting_weight, mixing_weight)
    return refined[None]


def solution(mesh):
    placed = (
        P("tm", "rows", None, None),
        P(None, None, "tm", "rows", None),
        P(None, None, "tm", "rows", None),
        P(None, "tm"),
        P(),
        P(),
    )
    return jax.shard_map(
        functools.partial(shards, mesh.shape["tm"], mesh.shape["rows"]),
        mesh=mesh,
        in_specs=placed,
        out_specs=P("tm", "rows", None, None),
        check_vma=False,
    )
```
